32 devices in a mesh: box: 8 (over y, x, core), copy: 4 (over z).
Axes of the slice: x: 2, y: 2, z: 4, core: 2. Of those that a mesh axis runs over, the one named last changes fastest.
Arguments:
- positions: float32 [2048, 3, 128], P(('copy', 'box')), parts along dimension 0, may hold values from 0 to 1
- charges: float32 [2048, 128], P(('copy', 'box')), parts along dimension 0, may hold values from -0.1875 to 0.1875
- counts: int32 [2048], P(('copy', 'box')), parts along dimension 0, may hold values from 1 to 128
- multipoles: float32 [2048, 121], P(('copy', 'box')), parts along dimension 0, may hold values from -6 to 6
- device_local: float32 [32, 121], P(('copy', 'box')), parts along dimension 0, may hold values from -6 to 6
- m2l_sources: int32 [2048, 16], P(('copy', 'box')), parts along dimension 0, may hold values from 0 to 511, as said below
- m2l_kinds: int32 [2048, 16], P(('copy', 'box')), parts along dimension 0, may hold values from 0 to 31, as said below
- m2l_ops: float32 [32, 121, 121], replicated, may hold values from -0.125 to 0.125
- l2l_ops: float32 [8, 121, 121], replicated, may hold values from -0.5 to 0.5
Outputs:
- near_potential: float32 [2048, 128], P(('copy', 'box')), parts along dimension 0
- leaf_local: float32 [2048, 121], P(('copy', 'box')), parts along dimension 0
The draws below stay inside these ranges and needn't reach their ends.
There are 4 independent parts, one for each index of `copy`. The reference program is written for one: setup_inputs(seed, part) draws one part's arguments, and reference() takes and returns one part's arrays. A program takes and returns all parts, laid end to end along the dimension named above; an argument that names none is the same for every part. Nothing has to cross between parts.
Inputs may be any that keep to these rules, and one draw needn't show every extreme that they name: `counts`: slots from the count on are padding. `m2l_sources`: the entries of a leaf are distinct children of boxes adjacent (periodically) to the leaf's parent, none adjacent to the leaf itself. `m2l_kinds`: entries with the same offset from source to target leaf have the same kind.
All inputs are finite; a program needn't handle non-finite values.
Results may differ from the reference program's by a relative error of at most 0.0003.
Values sent between devices are 32-bit elements; how exact they have to be, the bound alone decides.
A program may use at most 64 MiB of HBM per device.

```python
import jax
import jax.numpy as jnp
from jax import lax

TERMS = 121
P_SIZE = 128
LEAF_SIDE = 4
IL = 16
NOPS = 32
DGRID = 2
LEAF_DEV = 64
NL = 512
N_BOX = 8


def split_code_drawn(code_value, bit_count):
    coords_out = []
    for axis_id in range(3):
        result = jnp.zeros_like(code_value)
        for bit_id in range(bit_count):
            result = result + code_value // 2 ** (3 * bit_id + axis_id) % 2 * 2 ** bit_id
        coords_out.append(result)
    return coords_out


def join_code_drawn(coords_in, bit_count):
    result = jnp.zeros_like(coords_in[0])
    for axis_id in range(3):
        for bit_id in range(bit_count):
            result = result + coords_in[axis_id] // 2 ** bit_id % 2 * 2 ** (3 * bit_id + axis_id)
    return result


def far_lists(key):
    grid_bits = int(DGRID).bit_length() - 1
    side_bits = int(LEAF_SIDE).bit_length() - 1
    extent = DGRID * LEAF_SIDE
    leaf_ids = jnp.arange(NL, dtype=jnp.int32)
    box_coord = split_code_drawn(leaf_ids // LEAF_DEV, grid_bits)
    inner_coord = split_code_drawn(leaf_ids % LEAF_DEV, side_bits)
    placed = [box_coord[axis_id] * LEAF_SIDE + inner_coord[axis_id] for axis_id in range(3)]
    candidate = jnp.arange(216, dtype=jnp.int32)
    steps_in = [candidate // 36, candidate // 6 % 6, candidate % 6]
    deltas = [steps_in[axis_id][None, :] - 2 - placed[axis_id][:, None] % 2 for axis_id in range(3)]
    adjacent = (jnp.abs(deltas[0]) <= 1) & (jnp.abs(deltas[1]) <= 1) & (jnp.abs(deltas[2]) <= 1)
    scores = jax.random.randint(key, (NL, 216), 0, 2 ** 20, dtype=jnp.int32) * 256 + candidate[None, :]
    scores = jnp.where(adjacent, -1, scores)
    unused, chosen = lax.top_k(scores, IL)
    chosen = chosen.astype(jnp.int32)
    picked = [jnp.take_along_axis(deltas[axis_id], chosen, axis=1) for axis_id in range(3)]
    moved = [(placed[axis_id][:, None] + picked[axis_id]) % extent for axis_id in range(3)]
    owner_code = join_code_drawn([moved_coord // LEAF_SIDE for moved_coord in moved], grid_bits)
    inner_code = join_code_drawn([moved_coord % LEAF_SIDE for moved_coord in moved], side_bits)
    sources = (owner_code * LEAF_DEV + inner_code).astype(jnp.int32)
    kinds = (((picked[0] + 3) * 49 + (picked[1] + 3) * 7 + (picked[2] + 3)) % NOPS).astype(jnp.int32)
    return (sources, kinds)


def draw_m2l_sources(key, part):
    return far_lists(jax.random.fold_in(key, 11))[0]


def draw_m2l_kinds(key, part):
    return far_lists(jax.random.fold_in(key, 11))[1]


def touch_ends(entries, stream_key, low, top_value):
    longest = entries.shape.index(max(entries.shape))
    spots = []
    for shift in (0, 1):
        where = [jax.random.randint(jax.random.fold_in(stream_key, axis), (), 0, length) for axis, length in enumerate(entries.shape)]
        where[longest] = (where[longest] + shift) % entries.shape[longest]
        spots.append(tuple(where))
    return entries.at[spots[0]].set(low).at[spots[1]].set(top_value)


def level_of(key, dims, cuts, least, high):
    loudness, own = 1.0, jax.random.fold_in(key, 6)
    for position, shards_of in cuts:
        steps = jnp.exp(jax.random.uniform(jax.random.fold_in(own, position), (shards_of,), jnp.float32, least / len(cuts), high / len(cuts)))
        loudness = loudness * jnp.repeat(steps, dims[position] // shards_of).reshape([-1 if axis == position else 1 for axis in range(len(dims))])
    return loudness


def gaussian(rng, shape, width, limit, pieces=(), held_as=jnp.bfloat16):
    values = width * jax.random.normal(rng, shape, jnp.float32)
    if pieces:
        values = values * level_of(rng, shape, pieces, -0.22, 0.18)
    return jnp.clip(values, -limit, limit).astype(held_as)


def setup_inputs(seed: int = 0, part: int = 0) -> dict:
    seeds = jax.random.split(jax.random.key(seed), 10)
    part_keys = jax.random.split(jax.random.fold_in(seeds[9], part), 10)
    positions = jnp.clip(1.0 * jax.random.uniform(part_keys[0], (NL, 3, P_SIZE), jnp.float32) ** level_of(part_keys[0], (NL, 3, P_SIZE), ((0, 8),), -0.2, 0.2), 0.0, 1.0)
    charges = gaussian(part_keys[1], (NL, P_SIZE), 0.03, 0.1875, ((0, 8),), jnp.float32)
    counts = touch_ends(jax.random.randint(part_keys[2], (NL,), 1, P_SIZE + 1), jax.random.fold_in(part_keys[2], 1), 1, P_SIZE).astype(jnp.int32)
    multipoles = gaussian(part_keys[3], (NL, TERMS), 1.0, 6.0, ((0, 8),), jnp.float32)
    device_local = gaussian(part_keys[4], (N_BOX, TERMS), 1.0, 6.0, ((0, 8),), jnp.float32)
    m2l_sources = draw_m2l_sources(jax.random.fold_in(jax.random.fold_in(seeds[9], part), 71), part)
    m2l_kinds = draw_m2l_kinds(jax.random.fold_in(jax.random.fold_in(seeds[9], part), 71), part)
    m2l_ops = gaussian(seeds[7], (NOPS, TERMS, TERMS), (TERMS * IL) ** -0.5, 0.125, (), jnp.float32)
    l2l_ops = gaussian(seeds[8], (8, TERMS, TERMS), TERMS ** -0.5, 0.5, (), jnp.float32)
    return dict(positions=positions, charges=charges, counts=counts, multipoles=multipoles, device_local=device_local, m2l_sources=m2l_sources, m2l_kinds=m2l_kinds, m2l_ops=m2l_ops, l2l_ops=l2l_ops)


SOFTENING_SQ = 0.0025

def split_code(code_value, bit_count):
    coords_out = []
    for axis_id in range(3):
        result = jnp.zeros_like(code_value)
        for bit_id in range(bit_count):
            result = result + code_value // 2 ** (3 * bit_id + axis_id) % 2 * 2 ** bit_id
        coords_out.append(result)
    return coords_out

def join_code(coords_in, bit_count):
    result = jnp.zeros_like(coords_in[0])
    for axis_id in range(3):
        for bit_id in range(bit_count):
            result = result + coords_in[axis_id] // 2 ** bit_id % 2 * 2 ** (3 * bit_id + axis_id)
    return result

def neighbour_ids(leaf_ids, grid_count, leaf_side):
    grid_bits = grid_count.bit_length() - 1
    side_bits = leaf_side.bit_length() - 1
    per_box = leaf_side ** 3
    extent = grid_count * leaf_side
    box_coord = split_code(leaf_ids // per_box, grid_bits)
    inner_coord = split_code(leaf_ids % per_box, side_bits)
    placed = [box_coord[axis_id] * leaf_side + inner_coord[axis_id] for axis_id in range(3)]
    columns = []
    for offset_id in range(27):
        deltas = (offset_id // 9 - 1, offset_id // 3 % 3 - 1, offset_id % 3 - 1)
        moved = [(placed[axis_id] + deltas[axis_id]) % extent for axis_id in range(3)]
        owner_code = join_code([moved_coord // leaf_side for moved_coord in moved], grid_bits)
        inner_code = join_code([moved_coord % leaf_side for moved_coord in moved], side_bits)
        columns.append(owner_code * per_box + inner_code)
    return jnp.stack(columns, axis=-1).astype(jnp.int32)

def offset_table():
    rows_list = [[offset_id // 9 - 1, offset_id // 3 % 3 - 1, offset_id % 3 - 1] for offset_id in range(27)]
    return jnp.array(rows_list, dtype=jnp.float32)

def self_mask(tile_slots):
    slot_ids = jnp.arange(tile_slots)
    same_slot = slot_ids[:, None] == slot_ids[None, :]
    center = jnp.arange(27) == 13
    return center[:, None, None] & same_slot[None, :, :]

def block_potential(targets, sources, source_charge, offsets, excluded):
    dist_sq = jnp.zeros((targets.shape[0], 27, targets.shape[2], sources.shape[3]), jnp.float32)
    for axis_id in range(3):
        gap = offsets[None, :, axis_id, None, None] + sources[:, :, axis_id, None, :] - targets[:, None, axis_id, :, None]
        dist_sq = dist_sq + gap * gap
    inverse = jnp.where(excluded[None], 0.0, lax.rsqrt(dist_sq + SOFTENING_SQ))
    return jnp.einsum('bopq,boq->bp', inverse, source_charge, precision=lax.Precision.HIGHEST)

def reference(positions, charges, counts, multipoles, device_local, m2l_sources, m2l_kinds, m2l_ops, l2l_ops):
    live_mask = jnp.arange(P_SIZE)[None, :] < counts[:, None]
    charge_live = jnp.where(live_mask, charges, 0.0)
    neighbours = neighbour_ids(jnp.arange(NL, dtype=jnp.int32), DGRID, LEAF_SIDE)
    offsets = offset_table()
    excluded = self_mask(P_SIZE)

    def near_block(block_id):
        start = (block_id * 8).astype(jnp.int32)
        targets = lax.dynamic_slice_in_dim(positions, start, 8, 0)
        picked = lax.dynamic_slice_in_dim(neighbours, start, 8, 0)
        return block_potential(targets, positions[picked], charge_live[picked], offsets, excluded)
    near = lax.map(near_block, jnp.arange(NL // 8, dtype=jnp.int32)).reshape(NL, P_SIZE)
    near_potential = jnp.where(live_mask, near, 0.0)
    descended = device_local
    for step_id in range(LEAF_SIDE.bit_length() - 1):
        descended = jnp.einsum('cst,nt->ncs', l2l_ops, descended, precision=lax.Precision.HIGHEST).reshape(-1, TERMS)

    def translate_block(block_id):
        start = (block_id * 8).astype(jnp.int32)
        kinds = lax.dynamic_slice_in_dim(m2l_kinds, start, 8, 0)
        sources = lax.dynamic_slice_in_dim(m2l_sources, start, 8, 0)
        return jnp.einsum('best,bet->bs', m2l_ops[kinds], multipoles[sources], precision=lax.Precision.HIGHEST)
    far_terms = lax.map(translate_block, jnp.arange(NL // 8, dtype=jnp.int32)).reshape(NL, TERMS)
    leaf_local = descended + far_terms
    return (near_potential, leaf_local)
```

```python
import functools

import jax
import jax.numpy as jnp
from jax import lax
from jax.experimental import pallas as pl
from jax.experimental.pallas import tpu as pltpu
from jax.sharding import PartitionSpec as P

SOFTENING_SQ = 0.0025
BF, F32 = jnp.bfloat16, jnp.float32


def spread(coord, axis_id, bits):
    code = 0
    for k in range(bits):
        code = code | (((coord >> k) & 1) << (3 * k + axis_id))
    return code


def unspread(code, axis_id, bits):
    coord = 0
    for k in range(bits):
        coord = coord | (((code >> (3 * k + axis_id)) & 1) << k)
    return coord


def rounded(x):
    return x.astype(BF).astype(F32)


def pieces3(x):
    a = rounded(x)
    b = rounded(x - a)
    return a, b, x - a - b


def offset_of(o):
    return o // 9 - 1, o // 3 % 3 - 1, o % 3 - 1


def near_kernel(side, grid_count, pool, tiles, counts, out, a_s, n_s, q_s, t_s, c_s):
    me = lax.axis_index("box")
    side_bits, grid_bits = side.bit_length() - 1, grid_count.bit_length() - 1
    wide = side + 2
    extent = side * grid_count
    all_bits = side_bits + grid_bits
    origin = [unspread(me, a, grid_bits) * side for a in range(3)]

    row16 = lax.broadcasted_iota(jnp.int32, (16, 128), 0)
    row32 = lax.broadcasted_iota(jnp.int32, (32, 128), 0)
    off_col = [row32 // 9 - 1, row32 // 3 % 3 - 1, row32 % 3 - 1]
    off_col = [x.astype(F32) for x in off_col]
    off_sq = off_col[0] * off_col[0] + off_col[1] * off_col[1] + off_col[2] * off_col[2]

    for o in range(27):
        d = offset_of(o)
        c = jnp.where((row16 >= 6) & (row16 < 9), 1.0, 0.0)
        for a in range(3):
            c = jnp.where((row16 == a) | (row16 == 3 + a), float(d[a]), c)
        c_s[o] = c

    def prep_source(p, _):
        cell = (p // (wide * wide), p // wide % wide, p % wide)
        idx = 0
        for a in range(3):
            idx = idx | spread((origin[a] + cell[a] + extent - 1) & (extent - 1), a, all_bits)
        tile = pool[idx]
        s = tile[0:3] - 0.5
        s1 = rounded(s)
        s2 = rounded(s - s1)
        st = s1 + s2
        a_s[p] = jnp.concatenate([s1, s2, s1, s2, jnp.zeros((4, 128), F32)], axis=0).astype(BF)
        x, y, z = st[0:1], st[1:2], st[2:3]
        base = x * x + y * y + z * z + SOFTENING_SQ
        lin = off_col[0] * x + off_col[1] * y + off_col[2] * z
        n = base + (lin + lin + off_sq)
        n1, n2, n3 = pieces3(n)
        n_s[p, 0] = n1
        n_s[p, 1] = n2
        n_s[p, 2] = n3
        q_s[p] = tile[3:4]
        return 0

    lax.fori_loop(0, wide**3, prep_source, 0, unroll=4)

    def prep_target(g, _):
        tile = tiles[g]
        t = tile[0:3] - 0.5
        t1 = rounded(t)
        t2 = rounded(t - t1)
        tt = t1 + t2
        sq = tt[0:1] * tt[0:1] + tt[1:2] * tt[1:2] + tt[2:3] * tt[2:3]
        m1, m2, m3 = pieces3(sq)
        u1, u2 = -2.0 * t1, -2.0 * t2
        rows = jnp.concatenate(
            [u1, u1, u2, u2, jnp.zeros((4, 128), F32), u1, u2, m1, m2, m3,
             jnp.ones((3, 128), F32), jnp.zeros((4 + 96, 128), F32)], axis=0)
        t_s[g] = rows.T.astype(BF)[:, 0:32]
        return 0

    lax.fori_loop(0, side**3, prep_target, 0, unroll=2)

    lanes = lax.broadcasted_iota(jnp.int32, (128, 128), 1)
    eye = lanes == lax.broadcasted_iota(jnp.int32, (128, 128), 0)
    lane_row = lax.broadcasted_iota(jnp.int32, (1, 128), 1)

    def weights(p, o):
        b = c_s[o]
        b = jnp.where(row16 == 9, n_s[p, 0, o:o + 1], b)
        b = jnp.where(row16 == 10, n_s[p, 1, o:o + 1], b)
        b = jnp.where(row16 == 11, n_s[p, 2, o:o + 1], b)
        return jnp.concatenate([a_s[p], b.astype(BF)], axis=0)

    def leaf(g, _):
        c = [unspread(g, a, side_bits) + 1 for a in range(3)]
        center = (c[0] * wide + c[1]) * wide + c[2]
        t = t_s[g]
        acc = jnp.zeros((128, 128), F32)
        order = [13] + [o for o in range(27) if o != 13]
        for first in range(0, 27, 2):
            group = order[first:first + 2]
            ps = [center + (offset_of(o)[0] * wide + offset_of(o)[1]) * wide + offset_of(o)[2] for o in group]
            w = jnp.concatenate([weights(p, o) for p, o in zip(ps, group)], axis=1)
            d = jnp.dot(t, w, preferred_element_type=F32)
            inv = lax.rsqrt(d)
            for i, (p, o) in enumerate(zip(ps, group)):
                term = inv[:, 128 * i:128 * (i + 1)] * q_s[p]
                if o == 13:
                    term = jnp.where(eye, 0.0, term)
                acc = acc + term
        total = jnp.sum(acc.T, axis=0, keepdims=True)
        out[pl.ds(g, 1), :] = jnp.where(lane_row < counts[g], total, 0.0)
        return 0

    lax.fori_loop(0, side**3, leaf, 0)


def dot3(a, b):
    a1 = a.astype(BF)
    a2 = (a - a1.astype(F32)).astype(BF)
    b1 = b.astype(BF)
    b2 = (b - b1.astype(F32)).astype(BF)
    dims = (((1,), (1,)), ((), ()))
    mm = functools.partial(lax.dot_general, dimension_numbers=dims, preferred_element_type=F32)
    return mm(a1, b1) + (mm(a1, b2) + mm(a2, b1))


def far_kernel(levels, mult, sources, kinds, m2l, l2l, dev_local, out, g_s, k_s, x_s, d_s):
    leaves, entries = kinds.shape
    terms = mult.shape[1]
    nops = m2l.shape[0]
    for e in range(entries):
        k_s[e] = jnp.broadcast_to(kinds[:, e:e + 1], (leaves, terms))

    def fetch(g, _):
        for e in range(entries):
            g_s[e, pl.ds(g, 1), :] = mult[pl.ds(sources[g, e], 1), :]
        return 0

    lax.fori_loop(0, leaves, fetch, 0, unroll=2)

    step = 16
    for r in range(leaves // 8):
        rows = pl.ds(8 * r, 8)
        for kb in range(0, nops, step):
            acc = [jnp.zeros((8, terms), F32)] * step
            for e in range(entries):
                val, kind = g_s[e, rows], k_s[e, rows]
                acc = [a + jnp.where(kind == kb + i, val, 0.0) for i, a in enumerate(acc)]
            for i in range(step):
                x_s[kb + i, rows] = acc[i]

    cur = jnp.broadcast_to(dev_local[...].reshape(1, terms), (8, terms))
    count = 1
    for _ in range(levels):
        for c in range(8):
            r = dot3(cur, l2l[c])
            d_s[pl.ds(c, max(count, 1), stride=8), :] = r[0:count]
        count = count * 8
        cur = d_s[0:count]
    far = cur

    def op(k, acc):
        return acc + dot3(x_s[k], m2l[k])

    out[...] = lax.fori_loop(0, nops, op, far, unroll=4)


def local(
    positions, charges, counts, multipoles, device_local, m2l_sources, m2l_kinds, m2l_ops, l2l_ops
):
    box_count = lax.axis_size("box")
    per_box, _, slots = positions.shape
    terms = multipoles.shape[1]
    entries = m2l_kinds.shape[1]
    nops = m2l_ops.shape[0]
    side, grid_count, levels = 2, 2, 1
    while side**3 < per_box:
        side, levels = side * 2, levels + 1
    while grid_count**3 < box_count:
        grid_count *= 2
    cells = (side + 2) ** 3
    live = jnp.arange(slots)[None, :] < counts[:, None]
    tiles = jnp.concatenate([positions, jnp.where(live, charges, 0.0)[:, None, :]], axis=1)
    pool = lax.all_gather(tiles, "box", axis=0, tiled=True)
    all_mult = lax.all_gather(multipoles, "box", axis=0, tiled=True)
    vmem = pl.BlockSpec(memory_space=pltpu.VMEM)
    smem = pl.BlockSpec(memory_space=pltpu.SMEM)
    params = pltpu.CompilerParams(vmem_limit_bytes=50 * 2**20)
    near = pl.pallas_call(
        functools.partial(near_kernel, side, grid_count),
        out_shape=jax.ShapeDtypeStruct((per_box, slots), F32),
        in_specs=[vmem, vmem, smem],
        out_specs=vmem,
        scratch_shapes=[
            pltpu.VMEM((cells, 16, slots), BF),
            pltpu.VMEM((cells, 3, 32, slots), F32),
            pltpu.VMEM((cells, 1, slots), F32),
            pltpu.VMEM((per_box, slots, 32), BF),
            pltpu.VMEM((27, 16, slots), F32),
        ],
        compiler_params=params,
    )(pool, tiles, counts)
    leaf_local = pl.pallas_call(
        functools.partial(far_kernel, levels),
        out_shape=jax.ShapeDtypeStruct((per_box, terms), F32),
        in_specs=[vmem, smem, vmem, vmem, vmem, vmem],
        out_specs=vmem,
        scratch_shapes=[
            pltpu.VMEM((entries, per_box, terms), F32),
            pltpu.VMEM((entries, per_box, terms), jnp.int32),
            pltpu.VMEM((nops, per_box, terms), F32),
            pltpu.VMEM((per_box, terms), F32),
        ],
        compiler_params=params,
    )(all_mult, m2l_sources, m2l_kinds, m2l_ops, l2l_ops, device_local)
    return (near, leaf_local)


def solution(mesh):
    placed = (
        P(("copy", "box"), None, None),
        P(("copy", "box"), None),
        P(("copy", "box")),
        P(("copy", "box"), None),
        P(("copy", "box"), None),
        P(("copy", "box"), None),
        P(("copy", "box"), None),
        P(),
        P(),
    )
    return jax.shard_map(
        local,
        mesh=mesh,
        in_specs=placed,
        out_specs=(P(("copy", "box"), None), P(("copy", "box"), None)),
        check_vma=False,
    )
```

```python
import functools

import jax
import jax.numpy as jnp
from jax import lax
from jax.experimental import pallas as pl
from jax.experimental.pallas import tpu as pltpu
from jax.sharding import PartitionSpec as P

SOFTENING_SQ = 0.0025
BF, F32 = jnp.bfloat16, jnp.float32


def unspread(code, axis_id, bits):
    coord = 0
    for k in range(bits):
        coord = coord | (((code >> (3 * k + axis_id)) & 1) << k)
    return coord


def rounded(x):
    return x.astype(BF).astype(F32)


def pieces3(x):
    a = rounded(x)
    b = rounded(x - a)
    return a, b, x - a - b


def offset_of(o):
    return o // 9 - 1, o // 3 % 3 - 1, o % 3 - 1


def exchange_kernel(side, grid_count, pos, charges, counts, mult, grid, all_mult, s_tile, r_tile, s_mult, r_mult):
    me = lax.axis_index("box")
    grid_bits, side_bits = grid_count.bit_length() - 1, side.bit_length() - 1
    per_box, terms = mult.shape
    place = []
    for a in range(3):
        value = 0
        for k in range(grid_bits):
            value = value + lax.rem(lax.div(me, 2 ** (3 * k + a)), 2) * 2**k
        place.append(value)

    def device(d):
        code = 0
        for a in range(3):
            moved = lax.rem(place[a] + (d[a] + grid_count), grid_count)
            for k in range(grid_bits):
                code = code + lax.rem(lax.div(moved, 2**k), 2) * 2 ** (3 * k + a)
        return {"box": code}

    moves = [offset_of(o) for o in range(27) if o != 13]
    partners = [d for d in moves if grid_count > 2 or min(d) >= 0]
    barrier = pltpu.get_barrier_semaphore()
    for d in partners:
        pl.semaphore_signal(barrier, inc=1, device_id=device(d), device_id_type=pl.DeviceIdType.MESH)

    own = pl.ds(pl.multiple_of(me * per_box, per_box), per_box)
    all_mult[own, :] = jnp.concatenate([mult[...], jnp.zeros((per_box, 128 - terms), F32)], axis=1)
    lane_row = lax.broadcasted_iota(jnp.int32, (1, 128), 1)
    for m in range(per_box):
        x, y, z = (unspread(m, a, side_bits) + 1 for a in range(3))
        for a in range(3):
            grid[x, y, z, a:a + 1] = pos[a, m:m + 1]
        grid[x, y, z, 3:4] = jnp.where(lane_row < counts[m], charges[m:m + 1], 0.0)
    pl.semaphore_wait(barrier, len(partners))

    def part(d, at):
        return tuple(at(x) if x else slice(1, side + 1) for x in d)

    copies = []
    for i, d in enumerate(moves):
        src = part(d, lambda x: slice(side, side + 1) if x > 0 else slice(1, 2))
        dst = part(d, lambda x: slice(0, 1) if x > 0 else slice(side + 1, side + 2))
        copies.append(pltpu.make_async_remote_copy(
            src_ref=grid.at[src], dst_ref=grid.at[dst], send_sem=s_tile.at[i], recv_sem=r_tile.at[i],
            device_id=device(d), device_id_type=pl.DeviceIdType.MESH))
    for i, d in enumerate(partners):
        copies.append(pltpu.make_async_remote_copy(
            src_ref=all_mult.at[own], dst_ref=all_mult.at[own], send_sem=s_mult.at[i], recv_sem=r_mult.at[i],
            device_id=device(d), device_id_type=pl.DeviceIdType.MESH))
    for c in copies:
        c.start()
    for c in copies:
        c.wait()


def near_kernel(side, grid, counts, out, a_s, n_s, q_s, t_s, c_s):
    side_bits = side.bit_length() - 1
    wide = side + 2

    row16 = lax.broadcasted_iota(jnp.int32, (16, 128), 0)
    row32 = lax.broadcasted_iota(jnp.int32, (32, 128), 0)
    off_col = [row32 // 9 - 1, row32 // 3 % 3 - 1, row32 % 3 - 1]
    off_col = [x.astype(F32) for x in off_col]
    off_sq = off_col[0] * off_col[0] + off_col[1] * off_col[1] + off_col[2] * off_col[2]

    for o in range(27):
        d = offset_of(o)
        c = jnp.where((row16 >= 6) & (row16 < 9), 1.0, 0.0)
        for a in range(3):
            c = jnp.where((row16 == a) | (row16 == 3 + a), float(d[a]), c)
        c_s[o] = c

    def prep_source(p, _):
        tile = grid[p]
        s = tile[0:3] - 0.5
        s1 = rounded(s)
        s2 = rounded(s - s1)
        st = s1 + s2
        a_s[p] = jnp.concatenate([s1, s2, s1, s2, jnp.zeros((4, 128), F32)], axis=0).astype(BF)
        x, y, z = st[0:1], st[1:2], st[2:3]
        base = x * x + y * y + z * z + SOFTENING_SQ
        lin = off_col[0] * x + off_col[1] * y + off_col[2] * z
        n = base + (lin + lin + off_sq)
        n1, n2, n3 = pieces3(n)
        n_s[p, 0] = n1
        n_s[p, 1] = n2
        n_s[p, 2] = n3
        q_s[p] = tile[3:4]
        return 0

    lax.fori_loop(0, wide**3, prep_source, 0, unroll=8)

    def prep_target(g, _):
        c = [unspread(g, a, side_bits) + 1 for a in range(3)]
        t = grid[(c[0] * wide + c[1]) * wide + c[2]][0:3] - 0.5
        t1 = rounded(t)
        t2 = rounded(t - t1)
        tt = t1 + t2
        sq = tt[0:1] * tt[0:1] + tt[1:2] * tt[1:2] + tt[2:3] * tt[2:3]
        m1, m2, m3 = pieces3(sq)
        u1, u2 = -2.0 * t1, -2.0 * t2
        rows = jnp.concatenate(
            [u1, u1, u2, u2, jnp.zeros((4, 128), F32), u1, u2, m1, m2, m3,
             jnp.ones((3, 128), F32), jnp.zeros((4, 128), F32)], axis=0)
        t_s[g] = rows.T.astype(BF)
        return 0

    lax.fori_loop(0, side**3, prep_target, 0, unroll=8)

    lanes = lax.broadcasted_iota(jnp.int32, (128, 128), 1)
    eye = lanes == lax.broadcasted_iota(jnp.int32, (128, 128), 0)
    lane_row = lax.broadcasted_iota(jnp.int32, (1, 128), 1)

    def weights(p, o):
        b = c_s[o]
        b = jnp.where(row16 == 9, n_s[p, 0, o:o + 1], b)
        b = jnp.where(row16 == 10, n_s[p, 1, o:o + 1], b)
        b = jnp.where(row16 == 11, n_s[p, 2, o:o + 1], b)
        return jnp.concatenate([a_s[p], b.astype(BF)], axis=0)

    def leaf(g, _):
        c = [unspread(g, a, side_bits) + 1 for a in range(3)]
        center = (c[0] * wide + c[1]) * wide + c[2]
        t = t_s[g]
        acc = jnp.zeros((128, 128), F32)
        order = [13] + [o for o in range(27) if o != 13]
        for first in range(0, 27, 2):
            group = order[first:first + 2]
            ps = [center + (offset_of(o)[0] * wide + offset_of(o)[1]) * wide + offset_of(o)[2] for o in group]
            w = jnp.concatenate([weights(p, o) for p, o in zip(ps, group)], axis=1)
            d = jnp.dot(t, w, preferred_element_type=F32)
            inv = lax.rsqrt(d)
            for i, (p, o) in enumerate(zip(ps, group)):
                term = inv[:, 128 * i:128 * (i + 1)] * q_s[p]
                if o == 13:
                    term = jnp.where(eye, 0.0, term)
                acc = acc + term
        total = jnp.sum(acc.T, axis=0, keepdims=True)
        out[pl.ds(g, 1), :] = jnp.where(lane_row < counts[g], total, 0.0)
        return 0

    lax.fori_loop(0, side**3, leaf, 0, unroll=4)


def dot3(a, b):
    a1 = a.astype(BF)
    a2 = (a - a1.astype(F32)).astype(BF)
    b1 = b.astype(BF)
    b2 = (b - b1.astype(F32)).astype(BF)
    dims = (((1,), (1,)), ((), ()))
    mm = functools.partial(lax.dot_general, dimension_numbers=dims, preferred_element_type=F32)
    return mm(a1, b1) + (mm(a1, b2) + mm(a2, b1))


def far_kernel(levels, mult, sources, kinds, m2l, l2l, dev_local, out, g_s, k_s, x_s, d_s):
    leaves, entries = kinds.shape
    terms = out.shape[1]
    nops = m2l.shape[0]
    for e in range(entries):
        k_s[e] = jnp.broadcast_to(kinds[:, e:e + 1], (leaves, 128))

    def fetch(g, _):
        for e in range(entries):
            g_s[e, pl.ds(g, 1), :] = mult[pl.ds(sources[e, g], 1), :]
        return 0

    lax.fori_loop(0, leaves, fetch, 0, unroll=2)

    step = 16
    for r in range(leaves // 8):
        rows = pl.ds(8 * r, 8)
        for kb in range(0, nops, step):
            acc = [jnp.zeros((8, 128), F32)] * step
            for e in range(entries):
                val, kind = g_s[e, rows], k_s[e, rows]
                acc = [a + jnp.where(kind == kb + i, val, 0.0) for i, a in enumerate(acc)]
            for i in range(step):
                x_s[kb + i, rows] = acc[i]

    cur = jnp.broadcast_to(dev_local[...].reshape(1, terms), (8, terms))
    count = 1
    for _ in range(levels):
        for c in range(8):
            r = dot3(cur, l2l[c])
            d_s[pl.ds(c, max(count, 1), stride=8), :] = r[0:count]
        count = count * 8
        cur = d_s[0:count]
    far = cur

    def op(k, acc):
        return acc + dot3(x_s[k][:, 0:terms], m2l[k])

    out[...] = lax.fori_loop(0, nops, op, far, unroll=4)


def local(
    positions, charges, counts, multipoles, device_local, m2l_sources, m2l_kinds, m2l_ops, l2l_ops
):
    box_count = lax.axis_size("box")
    per_box, _, slots = positions.shape
    terms = multipoles.shape[1]
    entries = m2l_kinds.shape[1]
    nops = m2l_ops.shape[0]
    side, grid_count, levels = 2, 2, 1
    while side**3 < per_box:
        side, levels = side * 2, levels + 1
    while grid_count**3 < box_count:
        grid_count *= 2
    cells = (side + 2) ** 3
    vmem = pl.BlockSpec(memory_space=pltpu.VMEM)
    smem = pl.BlockSpec(memory_space=pltpu.SMEM)
    params = pltpu.CompilerParams(vmem_limit_bytes=50 * 2**20)
    partners = min(box_count, 27) - 1
    wide = side + 2
    grid, all_mult = pl.pallas_call(
        functools.partial(exchange_kernel, side, grid_count),
        out_shape=(
            jax.ShapeDtypeStruct((wide, wide, wide, 4, slots), F32),
            jax.ShapeDtypeStruct((box_count * per_box, 128), F32),
        ),
        in_specs=[vmem, vmem, smem, vmem],
        out_specs=(vmem, vmem),
        scratch_shapes=[
            pltpu.SemaphoreType.DMA((26,)),
            pltpu.SemaphoreType.DMA((26,)),
            pltpu.SemaphoreType.DMA((partners,)),
            pltpu.SemaphoreType.DMA((partners,)),
        ],
        compiler_params=pltpu.CompilerParams(collective_id=0, has_side_effects=True),
    )(positions.transpose(1, 0, 2), charges, counts, multipoles)
    near = pl.pallas_call(
        functools.partial(near_kernel, side),
        out_shape=jax.ShapeDtypeStruct((per_box, slots), F32),
        in_specs=[vmem, smem],
        out_specs=vmem,
        scratch_shapes=[
            pltpu.VMEM((cells, 16, slots), BF),
            pltpu.VMEM((cells, 3, 32, slots), F32),
            pltpu.VMEM((cells, 1, slots), F32),
            pltpu.VMEM((per_box, slots, 32), BF),
            pltpu.VMEM((27, 16, slots), F32),
        ],
        compiler_params=params,
    )(grid.reshape(cells, 4, slots), counts)
    leaf_local = pl.pallas_call(
        functools.partial(far_kernel, levels),
        out_shape=jax.ShapeDtypeStruct((per_box, terms), F32),
        in_specs=[vmem, smem, vmem, vmem, vmem, vmem],
        out_specs=vmem,
        scratch_shapes=[
            pltpu.VMEM((entries, per_box, 128), F32),
            pltpu.VMEM((entries, per_box, 128), jnp.int32),
            pltpu.VMEM((nops, per_box, 128), F32),
            pltpu.VMEM((per_box, terms), F32),
        ],
        compiler_params=params,
    )(all_mult, m2l_sources.T, m2l_kinds, m2l_ops, l2l_ops, device_local)
    return (near, leaf_local)


def solution(mesh):
    placed = (
        P(("copy", "box"), None, None),
        P(("copy", "box"), None),
        P(("copy", "box")),
        P(("copy", "box"), None),
        P(("copy", "box"), None),
        P(("copy", "box"), None),
        P(("copy", "box"), None),
        P(),
        P(),
    )
    return jax.shard_map(
        local,
        mesh=mesh,
        in_specs=placed,
        out_specs=(P(("copy", "box"), None), P(("copy", "box"), None)),
        check_vma=False,
    )
```

```python
import functools

import jax
import jax.numpy as jnp
from jax import lax
from jax.experimental import pallas as pl
from jax.experimental.pallas import tpu as pltpu
from jax.sharding import PartitionSpec as P

SOFTENING_SQ = 0.0025
BF, F32 = jnp.bfloat16, jnp.float32


def unspread(code, axis_id, bits):
    coord = 0
    for k in range(bits):
        coord = coord | (((code >> (3 * k + axis_id)) & 1) << k)
    return coord


def rounded(x):
    return x.astype(BF).astype(F32)


def pieces3(x):
    a = rounded(x)
    b = rounded(x - a)
    return a, b, x - a - b


def offset_of(o):
    return o // 9 - 1, o // 3 % 3 - 1, o % 3 - 1


def exchange_kernel(side, grid_count, pos, charges, counts, mult, grid, all_mult, s_tile, r_tile, s_mult, r_mult):
    me = lax.axis_index("box")
    grid_bits, side_bits = grid_count.bit_length() - 1, side.bit_length() - 1
    per_box, terms = mult.shape
    place = []
    for a in range(3):
        value = 0
        for k in range(grid_bits):
            value = value + lax.rem(lax.div(me, 2 ** (3 * k + a)), 2) * 2**k
        place.append(value)

    def device(d):
        code = 0
        for a in range(3):
            moved = lax.rem(place[a] + (d[a] + grid_count), grid_count)
            for k in range(grid_bits):
                code = code + lax.rem(lax.div(moved, 2**k), 2) * 2 ** (3 * k + a)
        return {"box": code}

    moves = [offset_of(o) for o in range(27) if o != 13]
    partners = [d for d in moves if grid_count > 2 or min(d) >= 0]
    barrier = pltpu.get_barrier_semaphore()
    for d in partners:
        pl.semaphore_signal(barrier, inc=1, device_id=device(d), device_id_type=pl.DeviceIdType.MESH)

    own = pl.ds(pl.multiple_of(me * per_box, per_box), per_box)
    all_mult[own, :] = jnp.concatenate([mult[...], jnp.zeros((per_box, 128 - terms), F32)], axis=1)
    lane_row = lax.broadcasted_iota(jnp.int32, (1, 128), 1)
    for m in range(per_box):
        x, y, z = (unspread(m, a, side_bits) + 1 for a in range(3))
        for a in range(3):
            grid[x, y, z, a:a + 1] = pos[a, m:m + 1]
        grid[x, y, z, 3:4] = jnp.where(lane_row < counts[m], charges[m:m + 1], 0.0)
    pl.semaphore_wait(barrier, len(partners))

    def part(d, at):
        return tuple(at(x) if x else slice(1, side + 1) for x in d)

    copies = []
    for i, d in enumerate(moves):
        src = part(d, lambda x: slice(side, side + 1) if x > 0 else slice(1, 2))
        dst = part(d, lambda x: slice(0, 1) if x > 0 else slice(side + 1, side + 2))
        copies.append(pltpu.make_async_remote_copy(
            src_ref=grid.at[src], dst_ref=grid.at[dst], send_sem=s_tile.at[i], recv_sem=r_tile.at[i],
            device_id=device(d), device_id_type=pl.DeviceIdType.MESH))
    for i, d in enumerate(partners):
        copies.append(pltpu.make_async_remote_copy(
            src_ref=all_mult.at[own], dst_ref=all_mult.at[own], send_sem=s_mult.at[i], recv_sem=r_mult.at[i],
            device_id=device(d), device_id_type=pl.DeviceIdType.MESH))
    for c in copies:
        c.start()
    for c in copies:
        c.wait()


def near_kernel(side, grid, counts, out, a_s, n_s, q_s, t_s, c_s):
    side_bits = side.bit_length() - 1
    wide = side + 2

    row16 = lax.broadcasted_iota(jnp.int32, (16, 128), 0)
    row32 = lax.broadcasted_iota(jnp.int32, (32, 128), 0)
    off_col = [row32 // 9 - 1, row32 // 3 % 3 - 1, row32 % 3 - 1]
    off_col = [x.astype(F32) for x in off_col]
    off_sq = off_col[0] * off_col[0] + off_col[1] * off_col[1] + off_col[2] * off_col[2]

    for o in range(27):
        d = offset_of(o)
        c = jnp.where((row16 >= 6) & (row16 < 9), 1.0, 0.0)
        for a in range(3):
            c = jnp.where((row16 == a) | (row16 == 3 + a), float(d[a]), c)
        c_s[o] = c

    def prep_source(p, _):
        tile = grid[p]
        s = tile[0:3] - 0.5
        s1 = rounded(s)
        s2 = rounded(s - s1)
        st = s1 + s2
        a_s[p] = jnp.concatenate([s1, s2, s1, s2, jnp.zeros((4, 128), F32)], axis=0).astype(BF)
        x, y, z = st[0:1], st[1:2], st[2:3]
        base = x * x + y * y + z * z + SOFTENING_SQ
        lin = off_col[0] * x + off_col[1] * y + off_col[2] * z
        n = base + (lin + lin + off_sq)
        n1, n2, n3 = pieces3(n)
        n_s[p, 0] = n1
        n_s[p, 1] = n2
        n_s[p, 2] = n3
        q_s[p] = tile[3:4]
        return 0

    lax.fori_loop(0, wide**3, prep_source, 0, unroll=8)

    def prep_target(g, _):
        c = [unspread(g, a, side_bits) + 1 for a in range(3)]
        t = grid[(c[0] * wide + c[1]) * wide + c[2]][0:3] - 0.5
        t1 = rounded(t)
        t2 = rounded(t - t1)
        tt = t1 + t2
        sq = tt[0:1] * tt[0:1] + tt[1:2] * tt[1:2] + tt[2:3] * tt[2:3]
        m1, m2, m3 = pieces3(sq)
        u1, u2 = -2.0 * t1, -2.0 * t2
        rows = jnp.concatenate(
            [u1, u1, u2, u2, jnp.zeros((4, 128), F32), u1, u2, m1, m2, m3,
             jnp.ones((3, 128), F32), jnp.zeros((4, 128), F32)], axis=0)
        t_s[g] = rows.T.astype(BF)
        return 0

    lax.fori_loop(0, side**3, prep_target, 0, unroll=8)

    lanes = lax.broadcasted_iota(jnp.int32, (128, 128), 1)
    eye = lanes == lax.broadcasted_iota(jnp.int32, (128, 128), 0)
    lane_row = lax.broadcasted_iota(jnp.int32, (1, 128), 1)

    def weights(p, o):
        b = c_s[o]
        b = jnp.where(row16 == 9, n_s[p, 0, o:o + 1], b)
        b = jnp.where(row16 == 10, n_s[p, 1, o:o + 1], b)
        b = jnp.where(row16 == 11, n_s[p, 2, o:o + 1], b)
        return jnp.concatenate([a_s[p], b.astype(BF)], axis=0)

    def leaf(g, _):
        c = [unspread(g, a, side_bits) + 1 for a in range(3)]
        center = (c[0] * wide + c[1]) * wide + c[2]
        t = t_s[g]
        acc = jnp.zeros((128, 128), F32)
        order = [13] + [o for o in range(27) if o != 13]
        for first in range(0, 27, 2):
            group = order[first:first + 2]
            ps = [center + (offset_of(o)[0] * wide + offset_of(o)[1]) * wide + offset_of(o)[2] for o in group]
            w = jnp.concatenate([weights(p, o) for p, o in zip(ps, group)], axis=1)
            d = jnp.dot(t, w, preferred_element_type=F32)
            inv = lax.rsqrt(d)
            for i, (p, o) in enumerate(zip(ps, group)):
                term = inv[:, 128 * i:128 * (i + 1)] * q_s[p]
                if o == 13:
                    term = jnp.where(eye, 0.0, term)
                acc = acc + term
        total = jnp.sum(acc.T, axis=0, keepdims=True)
        out[pl.ds(g, 1), :] = jnp.where(lane_row < counts[g], total, 0.0)
        return 0

    lax.fori_loop(0, side**3, leaf, 0, unroll=8)


def dot3(a, b):
    a1 = a.astype(BF)
    a2 = (a - a1.astype(F32)).astype(BF)
    b1 = b.astype(BF)
    b2 = (b - b1.astype(F32)).astype(BF)
    dims = (((1,), (1,)), ((), ()))
    mm = functools.partial(lax.dot_general, dimension_numbers=dims, preferred_element_type=F32)
    return mm(a1, b1) + (mm(a1, b2) + mm(a2, b1))


def far_kernel(levels, mult, sources, kinds, m2l, l2l, dev_local, out, g_s, k_s, x_s, d_s):
    leaves, entries = kinds.shape
    terms = out.shape[1]
    nops = m2l.shape[0]
    for e in range(entries):
        k_s[e] = jnp.broadcast_to(kinds[:, e:e + 1], (leaves, 128))

    def fetch(g, _):
        for e in range(entries):
            g_s[e, pl.ds(g, 1), :] = mult[pl.ds(sources[e, g], 1), :]
        return 0

    lax.fori_loop(0, leaves, fetch, 0, unroll=8)

    step = 16
    for r in range(leaves // 8):
        rows = pl.ds(8 * r, 8)
        for kb in range(0, nops, step):
            acc = [jnp.zeros((8, 128), F32)] * step
            for e in range(entries):
                val, kind = g_s[e, rows], k_s[e, rows]
                acc = [a + jnp.where(kind == kb + i, val, 0.0) for i, a in enumerate(acc)]
            for i in range(step):
                x_s[kb + i, rows] = acc[i]

    cur = jnp.broadcast_to(dev_local[...].reshape(1, terms), (8, terms))
    count = 1
    for _ in range(levels):
        for c in range(8):
            r = dot3(cur, l2l[c])
            d_s[pl.ds(c, max(count, 1), stride=8), :] = r[0:count]
        count = count * 8
        cur = d_s[0:count]
    far = cur

    def op(k, acc):
        return acc + dot3(x_s[k][:, 0:terms], m2l[k])

    out[...] = lax.fori_loop(0, nops, op, far, unroll=8)


def local(
    positions, charges, counts, multipoles, device_local, m2l_sources, m2l_kinds, m2l_ops, l2l_ops
):
    box_count = lax.axis_size("box")
    per_box, _, slots = positions.shape
    terms = multipoles.shape[1]
    entries = m2l_kinds.shape[1]
    nops = m2l_ops.shape[0]
    side, grid_count, levels = 2, 2, 1
    while side**3 < per_box:
        side, levels = side * 2, levels + 1
    while grid_count**3 < box_count:
        grid_count *= 2
    cells = (side + 2) ** 3
    vmem = pl.BlockSpec(memory_space=pltpu.VMEM)
    smem = pl.BlockSpec(memory_space=pltpu.SMEM)
    params = pltpu.CompilerParams(vmem_limit_bytes=50 * 2**20)
    partners = min(box_count, 27) - 1
    wide = side + 2
    grid, all_mult = pl.pallas_call(
        functools.partial(exchange_kernel, side, grid_count),
        out_shape=(
            jax.ShapeDtypeStruct((wide, wide, wide, 4, slots), F32),
            jax.ShapeDtypeStruct((box_count * per_box, 128), F32),
        ),
        in_specs=[vmem, vmem, smem, vmem],
        out_specs=(vmem, vmem),
        scratch_shapes=[
            pltpu.SemaphoreType.DMA((26,)),
            pltpu.SemaphoreType.DMA((26,)),
            pltpu.SemaphoreType.DMA((partners,)),
            pltpu.SemaphoreType.DMA((partners,)),
        ],
        compiler_params=pltpu.CompilerParams(collective_id=0, has_side_effects=True),
    )(positions.transpose(1, 0, 2), charges, counts, multipoles)
    near = pl.pallas_call(
        functools.partial(near_kernel, side),
        out_shape=jax.ShapeDtypeStruct((per_box, slots), F32),
        in_specs=[vmem, smem],
        out_specs=vmem,
        scratch_shapes=[
            pltpu.VMEM((cells, 16, slots), BF),
            pltpu.VMEM((cells, 3, 32, slots), F32),
            pltpu.VMEM((cells, 1, slots), F32),
            pltpu.VMEM((per_box, slots, 32), BF),
            pltpu.VMEM((27, 16, slots), F32),
        ],
        compiler_params=params,
    )(grid.reshape(cells, 4, slots), counts)
    leaf_local = pl.pallas_call(
        functools.partial(far_kernel, levels),
        out_shape=jax.ShapeDtypeStruct((per_box, terms), F32),
        in_specs=[vmem, smem, vmem, vmem, vmem, vmem],
        out_specs=vmem,
        scratch_shapes=[
            pltpu.VMEM((entries, per_box, 128), F32),
            pltpu.VMEM((entries, per_box, 128), jnp.int32),
            pltpu.VMEM((nops, per_box, 128), F32),
            pltpu.VMEM((per_box, terms), F32),
        ],
        compiler_params=params,
    )(all_mult, m2l_sources.T, m2l_kinds, m2l_ops, l2l_ops, device_local)
    return (near, leaf_local)


def solution(mesh):
    placed = (
        P(("copy", "box"), None, None),
        P(("copy", "box"), None),
        P(("copy", "box")),
        P(("copy", "box"), None),
        P(("copy", "box"), None),
        P(("copy", "box"), None),
        P(("copy", "box"), None),
        P(),
        P(),
    )
    return jax.shard_map(
        local,
        mesh=mesh,
        in_specs=placed,
        out_specs=(P(("copy", "box"), None), P(("copy", "box"), None)),
        check_vma=False,
    )
```
